32 devices in a mesh: row: 4 (over x, core), pair: 8 (over z, y).
Axes of the slice: x: 2, y: 2, z: 4, core: 2. Of those that a mesh axis runs over, the one named last changes fastest.
Arguments:
- weight: float32 [14336, 2048], P('row', 'pair'), may hold values from -300 to 300
- move_flags: int32 [2, 8], P(None, 'pair'), may hold values from 0 to 1
Outputs:
- columns: float32 [14336, 2048], P('row', 'pair')
- norm_ratios: float32 [2048], P('pair')
The draws below stay inside these ranges and needn't reach their ends.
All inputs are finite; a program needn't handle non-finite values.
Results may differ from the reference program's by a relative error of at most 0.0003.
Values sent between devices are 32-bit elements; how exact they have to be, the bound alone decides.
A program may use at most 64 MiB of HBM per device.

```python
import math
import jax
import jax.numpy as jnp
from jax import lax

BLOCK = 128
SWEEPS = 2
POLAR = 8
ROUNDS = 3
M = 14336
N = 2048
N_PAIR = 8


def draw_weight(key, part):
    key_entries = jax.random.fold_in(key, 11)
    key_columns = jax.random.fold_in(key, 23)
    key_rows = jax.random.fold_in(key, 37)
    position = jnp.arange(N, dtype=jnp.float32) / (N - 1)
    col_scale = jnp.exp(position * math.log(3.0) + jax.random.uniform(key_columns, (N,), jnp.float32, 0.0, math.log(2.0)))
    entries = jax.random.truncated_normal(key_entries, -5.0, 5.0, (M, N), jnp.float32)
    row_scale = jnp.exp(jax.random.uniform(key_rows, (M,), jnp.float32, 0.0, math.log(10.0)))
    return entries * row_scale[:, None] * col_scale[None, :]


def set_ends(result, own_key, smallest, high):
    shape = result.shape
    place = [jax.random.randint(jax.random.fold_in(own_key, axis), (), 0, shape[axis]) for axis in range(len(shape))]
    result = result.at[tuple(place)].set(smallest)
    longest = shape.index(max(shape))
    place[longest] = (place[longest] + 1) % shape[longest]
    return result.at[tuple(place)].set(high)


def setup_inputs(seed: int = 0) -> dict:
    streams_of = jax.random.split(jax.random.key(seed), 3)
    weight = draw_weight(jax.random.fold_in(streams_of[2], 71), 0)
    move_flags = set_ends(jax.random.randint(streams_of[1], (ROUNDS - 1, N_PAIR), 0, 2), jax.random.fold_in(streams_of[1], 1), 0, 1).astype(jnp.int32)
    return {"weight": weight, "move_flags": move_flags}


precise = lax.Precision.HIGHEST

def contract(left, right):
    return lax.dot_general(left, right, (((0,), (0,)), ((), ())), precision=precise, preferred_element_type=jnp.float32)

def orthogonal_iteration(gram_pair):
    rotation = jnp.eye(gram_pair.shape[0], dtype=jnp.float32)
    for sweep_index in range(SWEEPS):
        product = jnp.dot(gram_pair, rotation, precision=precise, preferred_element_type=jnp.float32)
        normal = contract(product, product)
        scaled = product / jnp.sqrt(jnp.sqrt(jnp.sum(normal * normal)))
        for polar_index in range(POLAR):
            inner = contract(scaled, scaled)
            scaled = 1.5 * scaled - 0.5 * jnp.dot(scaled, inner, precision=precise, preferred_element_type=jnp.float32)
        rotation = scaled
    return rotation

def rotate_slot(matrix):
    gram_pair = contract(matrix, matrix)
    return jnp.dot(matrix, orthogonal_iteration(gram_pair), precision=precise, preferred_element_type=jnp.float32)

def reference(weight, move_flags):
    slots = weight.reshape(M, N_PAIR, 2 * BLOCK).transpose(1, 0, 2)
    rotated = slots
    for round_index in range(ROUNDS):
        rotated = lax.map(rotate_slot, slots)
        if round_index + 1 < ROUNDS:
            first_half = rotated[:, :, :BLOCK]
            second_half = rotated[:, :, BLOCK:]
            lead_moves = (move_flags[round_index] == 1)[:, None, None]
            staying = jnp.where(lead_moves, second_half, first_half)
            moving = jnp.where(lead_moves, first_half, second_half)
            slots = jnp.concatenate([staying, jnp.roll(moving, 1, axis=0)], axis=2)
    final_layout = rotated.transpose(1, 0, 2).reshape(M, N)
    squares_total = jnp.sum(final_layout * final_layout)
    divisor = jnp.sqrt(squares_total / (M * N))
    columns = final_layout / divisor
    norm_ratios = jnp.sqrt(lax.optimization_barrier(jnp.sum(final_layout * final_layout, axis=0)) / M) / divisor
    return (columns, norm_ratios)
```

```python
import functools

import jax
import jax.numpy as jnp
from jax import lax
from jax.experimental import pallas as pl
from jax.experimental.pallas import tpu as pltpu
from jax.sharding import PartitionSpec as P

SWEEPS = 2
POLAR = 8
ROUNDS = 3

MESH = pl.DeviceIdType.MESH
precise = lax.Precision.HIGH


def from_behind(block, axis, distance):
    devices = range(lax.axis_size(axis))
    route = [((i - distance) % len(devices), i) for i in devices]
    return lax.ppermute(block, axis, route)


def contract(left, right):
    return lax.dot_general(
        left, right, (((0,), (0,)), ((), ())), precision=precise, preferred_element_type=jnp.float32
    )


def times(left, right):
    return jnp.dot(left, right, precision=precise, preferred_element_type=jnp.float32)


def halves(value):
    high = value.astype(jnp.bfloat16)
    low = (value - high.astype(jnp.float32)).astype(jnp.bfloat16)
    return high, low


def product3(left, right):
    dot = functools.partial(jnp.dot, preferred_element_type=jnp.float32)
    return dot(left[0], right[0]) + (dot(left[0], right[1]) + dot(left[1], right[0]))


def iterate(gram):
    gram_parts = halves(gram)
    product = gram
    for sweep in range(SWEEPS):
        if sweep:
            product = product3(gram_parts, halves(product))
        parts = halves(product)
        normal = product3(parts, parts)
        scaled = product / jnp.sqrt(jnp.sqrt(jnp.sum(normal * normal)))

        def step(_, value):
            own = halves(value)
            inner = product3(own, own)
            return 1.5 * value - 0.5 * product3(own, halves(inner))

        product = lax.fori_loop(0, POLAR, step, scaled)
    return product


def solve_kernel(n, part, gram, basis, arrived, send1, recv1, send2, recv2):
    chunk = part.shape[0] // n
    me = lax.axis_index("row")
    others = [lax.rem(me + k, n) for k in range(1, n)]

    barrier = pltpu.get_barrier_semaphore()
    for other in others:
        pl.semaphore_signal(barrier, inc=1, device_id={"row": other}, device_id_type=MESH)
    pl.semaphore_wait(barrier, n - 1)

    copies = []
    for k, other in enumerate(others):
        copies.append(
            pltpu.make_async_remote_copy(
                src_ref=part.at[pl.ds(pl.multiple_of(other * chunk, chunk), chunk)],
                dst_ref=arrived.at[k],
                send_sem=send1.at[k],
                recv_sem=recv1.at[k],
                device_id={"row": other},
                device_id_type=MESH,
            )
        )
        copies[-1].start()
    mine = pl.ds(pl.multiple_of(me * chunk, chunk), chunk)
    total = part[mine, :]
    for k, copy in enumerate(copies):
        copy.wait_recv()
        total = total + arrived[k]
    gram[mine, :] = total
    spreads = []
    for k, other in enumerate(others):
        spreads.append(
            pltpu.make_async_remote_copy(
                src_ref=gram.at[mine],
                dst_ref=gram.at[mine],
                send_sem=send2.at[k],
                recv_sem=recv2.at[k],
                device_id={"row": other},
                device_id_type=MESH,
            )
        )
        spreads[-1].start()
    for copy in spreads:
        copy.wait_recv()
    for copy in copies + spreads:
        copy.wait_send()
    basis[...] = iterate(gram[...])


def solve(part):
    n = lax.axis_size("row")
    order = part.shape[0]
    dma = pltpu.SemaphoreType.DMA((n - 1,))
    vmem = pl.BlockSpec(memory_space=pltpu.VMEM)
    return pl.pallas_call(
        functools.partial(solve_kernel, n),
        out_shape=[jax.ShapeDtypeStruct(part.shape, jnp.float32)] * 2,
        in_specs=[vmem],
        out_specs=[vmem, vmem],
        scratch_shapes=[
            pltpu.VMEM((n - 1, order // n, order), jnp.float32),
            dma,
            dma,
            dma,
            dma,
        ],
        compiler_params=pltpu.CompilerParams(
            collective_id=0, has_side_effects=True, vmem_limit_bytes=16 * 1024 * 1024
        ),
        cost_estimate=pl.CostEstimate(
            flops=35 * 6 * order**3, bytes_accessed=12 * order * order, transcendentals=0
        ),
    )(part)


def on_device(weight, move_flags):
    half_width = weight.shape[1] // 2
    row_count = weight.shape[0] * lax.axis_size("row")
    cell_count = row_count * weight.shape[1] * lax.axis_size("pair")
    current = weight
    part = contract(current, current)
    for round_index in range(ROUNDS):
        gram, basis = solve(part)
        if round_index + 1 == ROUNDS:
            break
        lead, tail = basis[:, :half_width], basis[:, half_width:]
        lead_moves = move_flags[round_index, 0] == 1
        moving = times(current, jnp.where(lead_moves, lead, tail))
        arrived = from_behind(moving, "pair", 1)
        staying = times(current, jnp.where(lead_moves, tail, lead))
        corner = contract(staying, staying)
        cross = contract(staying, arrived)
        part = jnp.block([[corner, cross], [cross.T, contract(arrived, arrived)]])
        current = jnp.concatenate([staying, arrived], axis=1)
    squares = jnp.sum(basis * times(gram, basis), axis=0)
    squares_total = lax.psum(jnp.sum(squares), "pair")
    divisor = jnp.sqrt(squares_total / cell_count)
    columns = times(current, basis) / divisor
    norm_ratios = jnp.sqrt(squares / row_count) / divisor
    return (columns, norm_ratios)


def solution(mesh):
    return jax.shard_map(
        on_device,
        mesh=mesh,
        in_specs=(P("row", "pair"), P(None, "pair")),
        out_specs=(P("row", "pair"), P("pair")),
        check_vma=False,
    )
```

```python
import functools

import jax
import jax.numpy as jnp
from jax import lax
from jax.experimental import pallas as pl
from jax.experimental.pallas import tpu as pltpu
from jax.sharding import PartitionSpec as P

SWEEPS = 2
POLAR = 8
ROUNDS = 3

MESH = pl.DeviceIdType.MESH
precise = lax.Precision.HIGH


def from_behind(block, axis, distance):
    devices = range(lax.axis_size(axis))
    route = [((i - distance) % len(devices), i) for i in devices]
    return lax.ppermute(block, axis, route)


def contract(left, right):
    return lax.dot_general(
        left, right, (((0,), (0,)), ((), ())), precision=precise, preferred_element_type=jnp.float32
    )


def times(left, right):
    return jnp.dot(left, right, precision=precise, preferred_element_type=jnp.float32)


def halves(value):
    high = value.astype(jnp.bfloat16)
    low = (value - high.astype(jnp.float32)).astype(jnp.bfloat16)
    return high, low


def product3(left, right):
    dot = functools.partial(jnp.dot, preferred_element_type=jnp.float32)
    return dot(left[0], right[0]) + (dot(left[0], right[1]) + dot(left[1], right[0]))


def iterate(grams):
    values = grams
    for sweep in range(SWEEPS):
        if sweep:
            values = [product3(halves(g), halves(v)) for g, v in zip(grams, values)]
        scaled = []
        for value in values:
            parts = halves(value)
            normal = product3(parts, parts)
            scaled.append(value / jnp.sqrt(jnp.sqrt(jnp.sum(normal * normal))))

        def step(_, state):
            owns = [halves(value) for value in state]
            inners = [halves(product3(own, own)) for own in owns]
            cubes = [product3(own, inner) for own, inner in zip(owns, inners)]
            return tuple(1.5 * value - 0.5 * cube for value, cube in zip(state, cubes))

        values = lax.fori_loop(0, POLAR, step, tuple(scaled))
    return values


def send(source, target, semaphores, index, device):
    copy = pltpu.make_async_remote_copy(
        src_ref=source,
        dst_ref=target,
        send_sem=semaphores[0].at[index],
        recv_sem=semaphores[1].at[index],
        device_id=device,
        device_id_type=MESH,
    )
    copy.start()
    return copy


def solve_kernel(n, n_pair, whole, final, part, *refs):
    gram, basis = refs[:2]
    refs = refs[2:]
    if final:
        squares_ref, total_ref = refs[:2]
        refs = refs[2:]
    arrived, send1, recv1, send2, recv2 = refs[:5]
    chunk = part.shape[-1] // n
    row, pair = lax.axis_index("row"), lax.axis_index("pair")
    side = lax.rem(pair, 2)
    mate = pair + 1 - 2 * side
    in_row = [(lax.rem(row + k, n), pair, side) for k in range(1, n)]
    in_mate = [(lax.rem(row + k, n), mate, 1 - side) for k in range(n)]
    group = in_row + in_mate
    others = [lax.rem(pair + k, n_pair) for k in range(1, n_pair)]
    others = others if final else []

    barrier = pltpu.get_barrier_semaphore()
    for r, p, _ in group:
        pl.semaphore_signal(barrier, inc=1, device_id={"row": r, "pair": p}, device_id_type=MESH)
    for p in others:
        pl.semaphore_signal(barrier, inc=1, device_id={"pair": p}, device_id_type=MESH)
    pl.semaphore_wait(barrier, len(group) + len(others))

    def rows_of(r):
        return pl.ds(pl.multiple_of(r * chunk, chunk), chunk)

    copies = []
    for k, (r, p, s) in enumerate(in_row if whole else group):
        source = part.at[rows_of(r)] if whole else part.at[s, rows_of(r)]
        copies.append(send(source, arrived.at[k], (send1, recv1), k, {"row": r, "pair": p}))
    mine = rows_of(row)
    total = part[mine, :] if whole else part[side, mine, :]
    for k, copy in enumerate(copies):
        copy.wait_recv()
        total = total + arrived[k]
    gram[side, mine, :] = total
    spreads = []
    for k, (r, p, s) in enumerate(in_row if final else group):
        place = gram.at[side, mine]
        spreads.append(send(place, place, (send2, recv2), k, {"row": r, "pair": p}))
    for copy in spreads:
        copy.wait_recv()
    for copy in copies + spreads:
        copy.wait_send()
    if not final:
        basis[0], basis[1] = iterate([gram[0], gram[1]])
        return
    own = gram[side]
    (solved,) = iterate([own])
    basis[...] = solved
    squares = jnp.sum(solved * product3(halves(own), halves(solved)), axis=0, keepdims=True)
    squares_ref[...] = squares
    sent, landed, send3, recv3 = refs[5:]
    sent[...] = jnp.broadcast_to(jnp.sum(squares), sent.shape)
    traces = []
    for k, p in enumerate(others):
        traces.append(send(sent, landed.at[k], (send3, recv3), k, {"pair": p}))
    value = sent[...]
    for k, copy in enumerate(traces):
        copy.wait_recv()
        value = value + landed[k]
    total_ref[...] = value
    for copy in traces:
        copy.wait_send()


def solve(part, round_index):
    n, n_pair = lax.axis_size("row"), lax.axis_size("pair")
    order = part.shape[-1]
    whole, final = round_index == 0, round_index + 1 == ROUNDS
    dma = pltpu.SemaphoreType.DMA((2 * n - 1,))
    vmem = pl.BlockSpec(memory_space=pltpu.VMEM)
    both = jax.ShapeDtypeStruct((2, order, order), jnp.float32)
    shapes = [both, both]
    scratch = [pltpu.VMEM((2 * n - 1, order // n, order), jnp.float32), dma, dma, dma, dma]
    if final:
        shapes = [
            both,
            jax.ShapeDtypeStruct((order, order), jnp.float32),
            jax.ShapeDtypeStruct((1, order), jnp.float32),
            jax.ShapeDtypeStruct((8, 128), jnp.float32),
        ]
        far = pltpu.SemaphoreType.DMA((n_pair - 1,))
        scratch += [
            pltpu.VMEM((8, 128), jnp.float32),
            pltpu.VMEM((n_pair - 1, 8, 128), jnp.float32),
            far,
            far,
        ]
    return pl.pallas_call(
        functools.partial(solve_kernel, n, n_pair, whole, final),
        out_shape=shapes,
        in_specs=[vmem],
        out_specs=[vmem] * len(shapes),
        scratch_shapes=scratch,
        compiler_params=pltpu.CompilerParams(
            collective_id=round_index, has_side_effects=True, vmem_limit_bytes=24 * 1024 * 1024
        ),
        cost_estimate=pl.CostEstimate(
            flops=35 * 6 * order**3, bytes_accessed=60 * 1024 * 1024, transcendentals=0
        ),
    )(part)


def with_mate(block):
    devices = range(lax.axis_size("pair"))
    return lax.ppermute(block, "pair", [(i, i ^ 1) for i in devices])


def on_device(weight, move_flags):
    width = weight.shape[1]
    half_width = width // 2
    half_rows = weight.shape[0] // 2
    row_count = weight.shape[0] * lax.axis_size("row")
    cell_count = row_count * width * lax.axis_size("pair")
    pair = lax.axis_index("pair")
    left_side = pair % 2 == 0

    def by_side(here, there):
        return jnp.where(left_side, here, there), jnp.where(left_side, there, here)

    kept, given = by_side(weight[:half_rows], weight[half_rows:])
    pieces = 2
    step = half_rows // pieces
    spans = [slice(i * step, (i + 1) * step) for i in range(pieces)]
    received = [with_mate(given[span]) for span in spans]
    couples = [by_side(kept[span], got) for span, got in zip(spans, received)]

    part = contract(weight, weight)
    flags = jnp.concatenate(by_side(move_flags, with_mate(move_flags)), axis=1)
    for round_index in range(ROUNDS - 1):
        _, bases = solve(part, round_index)
        split = []
        for s in range(2):
            lead, tail = bases[s, :, :half_width], bases[s, :, half_width:]
            lead_moves = flags[round_index, s] == 1
            split.append((jnp.where(lead_moves, tail, lead), jnp.where(lead_moves, lead, tail)))
        last = round_index + 2 == ROUNDS
        next_couples, part, home = [], 0.0, []
        for even, odd in couples:
            moving = times(odd, split[1][1])
            came = from_behind(moving, "pair", 2)
            even_stay = times(even, split[0][0])
            odd_stay = times(odd, split[1][0])
            over = times(even, split[0][1])
            if last:
                stays = by_side(even_stay, odd_stay)
                home.append((stays[0], with_mate(stays[1])))
            grams = []
            for stay, move in ((even_stay, came), (odd_stay, over)):
                cross = contract(stay, move)
                grams.append(jnp.block([[contract(stay, stay), cross], [cross.T, contract(move, move)]]))
            part = part + jnp.stack(grams)
            if last:
                moves = by_side(came, over)
                home[-1] += (moves[0], with_mate(moves[1]))
            else:
                next_couples.append(
                    (
                        jnp.concatenate([even_stay, came], axis=1),
                        jnp.concatenate([odd_stay, over], axis=1),
                    )
                )
        couples = next_couples
    _, basis, squares, total = solve(part, ROUNDS - 1)
    divisor = jnp.sqrt(total[0, 0] / cell_count)
    own = [jnp.concatenate([h[0], h[2]], axis=1) for h in home]
    mates = [jnp.concatenate([h[1], h[3]], axis=1) for h in home]
    own, mates = jnp.concatenate(own, axis=0), jnp.concatenate(mates, axis=0)
    current = jnp.concatenate(by_side(own, mates), axis=0)
    columns = times(current, basis) / divisor
    norm_ratios = jnp.sqrt(squares[0] / row_count) / divisor
    return (columns, norm_ratios)


def solution(mesh):
    return jax.shard_map(
        on_device,
        mesh=mesh,
        in_specs=(P("row", "pair"), P(None, "pair")),
        out_specs=(P("row", "pair"), P("pair")),
        check_vma=False,
    )
```

```python
import functools

import jax
import jax.numpy as jnp
from jax import lax
from jax.experimental import pallas as pl
from jax.experimental.pallas import tpu as pltpu
from jax.sharding import PartitionSpec as P

SWEEPS = 2
POLAR = 8
ROUNDS = 3

MESH = pl.DeviceIdType.MESH
precise = lax.Precision.HIGH


def from_behind(block, axis, distance):
    devices = range(lax.axis_size(axis))
    route = [((i - distance) % len(devices), i) for i in devices]
    return lax.ppermute(block, axis, route)


def contract(left, right):
    return lax.dot_general(
        left, right, (((0,), (0,)), ((), ())), precision=precise, preferred_element_type=jnp.float32
    )


def times(left, right):
    return jnp.dot(left, right, precision=precise, preferred_element_type=jnp.float32)


def halves(value):
    high = value.astype(jnp.bfloat16)
    low = (value - high.astype(jnp.float32)).astype(jnp.bfloat16)
    return high, low


def product3(left, right):
    return jnp.dot(
        jnp.concatenate([left[0], left[0], left[1]], axis=1),
        jnp.concatenate([right[0], right[1], right[0]], axis=0),
        preferred_element_type=jnp.float32,
    )


def iterate(gram):
    gram_parts = halves(gram)
    product = gram
    for sweep in range(SWEEPS):
        if sweep:
            product = product3(gram_parts, halves(product))
        parts = halves(product)
        normal = product3(parts, parts)
        scaled = product / jnp.sqrt(jnp.sqrt(jnp.sum(normal * normal)))

        def step(_, value):
            own = halves(value)
            inner = product3(own, own)
            return 1.5 * value - 0.5 * product3(own, halves(inner))

        product = lax.fori_loop(0, POLAR, step, scaled)
    return product


def send(source, target, semaphores, index, device):
    copy = pltpu.make_async_remote_copy(
        src_ref=source,
        dst_ref=target,
        send_sem=semaphores[0].at[index],
        recv_sem=semaphores[1].at[index],
        device_id=device,
        device_id_type=MESH,
    )
    copy.start()
    return copy


def solve_kernel(n, n_pair, final, part, gram, basis, *refs):
    if final:
        squares_ref, total_ref = refs[:2]
        refs = refs[2:]
    arrived, send1, recv1, send2, recv2 = refs[:5]
    chunk = part.shape[0] // n
    me = lax.axis_index("row")
    others = [lax.rem(me + k, n) for k in range(1, n)]

    pair = lax.axis_index("pair")
    slots = [lax.rem(pair + k, n_pair) for k in range(1, n_pair)] if final else []

    barrier = pltpu.get_barrier_semaphore()
    for other in others:
        pl.semaphore_signal(barrier, inc=1, device_id={"row": other}, device_id_type=MESH)
    for slot in slots:
        pl.semaphore_signal(barrier, inc=1, device_id={"pair": slot}, device_id_type=MESH)
    pl.semaphore_wait(barrier, len(others) + len(slots))

    copies = []
    for k, other in enumerate(others):
        source = part.at[pl.ds(pl.multiple_of(other * chunk, chunk), chunk)]
        copies.append(send(source, arrived.at[k], (send1, recv1), k, {"row": other}))
    mine = pl.ds(pl.multiple_of(me * chunk, chunk), chunk)
    total = part[mine, :]
    for k, copy in enumerate(copies):
        copy.wait_recv()
        total = total + arrived[k]
    gram[mine, :] = total
    spreads = []
    for k, other in enumerate(others):
        spreads.append(send(gram.at[mine], gram.at[mine], (send2, recv2), k, {"row": other}))
    for copy in spreads:
        copy.wait_recv()
    for copy in copies + spreads:
        copy.wait_send()
    own = gram[...]
    solved = iterate(own)
    basis[...] = solved
    if not final:
        return
    squares = jnp.sum(solved * product3(halves(own), halves(solved)), axis=0, keepdims=True)
    squares_ref[...] = squares
    sent, landed, send3, recv3 = refs[5:]
    sent[...] = jnp.broadcast_to(jnp.sum(squares), sent.shape)
    traces = []
    for k, slot in enumerate(slots):
        traces.append(send(sent, landed.at[k], (send3, recv3), k, {"pair": slot}))
    value = sent[...]
    for k, copy in enumerate(traces):
        copy.wait_recv()
        value = value + landed[k]
    total_ref[...] = value
    for copy in traces:
        copy.wait_send()


def solve(part, final):
    n, n_pair = lax.axis_size("row"), lax.axis_size("pair")
    order = part.shape[0]
    dma = pltpu.SemaphoreType.DMA((n - 1,))
    vmem = pl.BlockSpec(memory_space=pltpu.VMEM)
    shapes = [jax.ShapeDtypeStruct(part.shape, jnp.float32)] * 2
    scratch = [pltpu.VMEM((n - 1, order // n, order), jnp.float32), dma, dma, dma, dma]
    if final:
        shapes += [
            jax.ShapeDtypeStruct((1, order), jnp.float32),
            jax.ShapeDtypeStruct((8, 128), jnp.float32),
        ]
        far = pltpu.SemaphoreType.DMA((n_pair - 1,))
        scratch += [
            pltpu.VMEM((8, 128), jnp.float32),
            pltpu.VMEM((n_pair - 1, 8, 128), jnp.float32),
            far,
            far,
        ]
    return pl.pallas_call(
        functools.partial(solve_kernel, n, n_pair, final),
        out_shape=shapes,
        in_specs=[vmem],
        out_specs=[vmem] * len(shapes),
        scratch_shapes=scratch,
        compiler_params=pltpu.CompilerParams(
            collective_id=int(final), has_side_effects=True, vmem_limit_bytes=16 * 1024 * 1024
        ),
        cost_estimate=pl.CostEstimate(
            flops=35 * 6 * order**3, bytes_accessed=40 * 1024 * 1024, transcendentals=0
        ),
    )(part)


def on_device(weight, move_flags):
    half_width = weight.shape[1] // 2
    row_count = weight.shape[0] * lax.axis_size("row")
    cell_count = row_count * weight.shape[1] * lax.axis_size("pair")
    current = weight
    part = contract(current, current)
    for round_index in range(ROUNDS):
        final = round_index + 1 == ROUNDS
        gram, basis, *sums = solve(part, final)
        if final:
            break
        lead, tail = basis[:, :half_width], basis[:, half_width:]
        lead_moves = move_flags[round_index, 0] == 1
        moving = times(current, jnp.where(lead_moves, lead, tail))
        arrived = from_behind(moving, "pair", 1)
        staying = times(current, jnp.where(lead_moves, tail, lead))
        corner = contract(staying, staying)
        current = jnp.concatenate([staying, arrived], axis=1)
        edge = contract(current, arrived)
        part = jnp.concatenate(
            [jnp.concatenate([corner, edge[:half_width].T], axis=0), edge], axis=1
        )
    squares, squares_total = sums[0][0], sums[1][0, 0]
    divisor = jnp.sqrt(squares_total / cell_count)
    columns = times(current, basis) / divisor
    norm_ratios = jnp.sqrt(squares / row_count) / divisor
    return (columns, norm_ratios)


def solution(mesh):
    return jax.shard_map(
        on_device,
        mesh=mesh,
        in_specs=(P("row", "pair"), P(None, "pair")),
        out_specs=(P("row", "pair"), P("pair")),
        check_vma=False,
    )
```

```python
import functools

import jax
import jax.numpy as jnp
from jax import lax
from jax.experimental import pallas as pl
from jax.experimental.pallas import tpu as pltpu
from jax.sharding import PartitionSpec as P

SWEEPS = 2
POLAR = 8
ROUNDS = 3

MESH = pl.DeviceIdType.MESH
precise = lax.Precision.HIGH


def from_behind(block, axis, distance):
    devices = range(lax.axis_size(axis))
    route = [((i - distance) % len(devices), i) for i in devices]
    return lax.ppermute(block, axis, route)


def contract(left, right):
    return lax.dot_general(
        left, right, (((0,), (0,)), ((), ())), precision=precise, preferred_element_type=jnp.float32
    )


def times(left, right):
    return jnp.dot(left, right, precision=precise, preferred_element_type=jnp.float32)


def halves(value):
    high = value.astype(jnp.bfloat16)
    low = (value - high.astype(jnp.float32)).astype(jnp.bfloat16)
    return high, low


def product3(left, right):
    return jnp.dot(
        jnp.concatenate([left[0], left[0], left[1]], axis=1),
        jnp.concatenate([right[0], right[1], right[0]], axis=0),
        preferred_element_type=jnp.float32,
    )


def iterate(gram):
    gram_parts = halves(gram)
    product = gram
    for sweep in range(SWEEPS):
        if sweep:
            product = product3(gram_parts, halves(product))
        parts = halves(product)
        normal = product3(parts, parts)
        scaled = product / jnp.sqrt(jnp.sqrt(jnp.sum(normal * normal)))

        def step(_, value):
            own = halves(value)
            inner = product3(own, own)
            return 1.5 * value - 0.5 * product3(own, halves(inner))

        product = lax.fori_loop(0, POLAR, step, scaled)
    return product


def send(source, target, semaphores, index, device):
    copy = pltpu.make_async_remote_copy(
        src_ref=source,
        dst_ref=target,
        send_sem=semaphores[0].at[index],
        recv_sem=semaphores[1].at[index],
        device_id=device,
        device_id_type=MESH,
    )
    copy.start()
    return copy


def solve_kernel(n, n_pair, final, part, gram, basis, *refs):
    if final:
        squares_ref, total_ref = refs[:2]
        refs = refs[2:]
    arrived, send1, recv1, send2, recv2 = refs[:5]
    chunk = part.shape[0] // n
    me = lax.axis_index("row")
    others = [lax.rem(me + k, n) for k in range(1, n)]

    pair = lax.axis_index("pair")
    slots = [lax.rem(pair + k, n_pair) for k in range(1, n_pair)] if final else []

    barrier = pltpu.get_barrier_semaphore()
    for other in others:
        pl.semaphore_signal(barrier, inc=1, device_id={"row": other}, device_id_type=MESH)
    for slot in slots:
        pl.semaphore_signal(barrier, inc=1, device_id={"pair": slot}, device_id_type=MESH)
    pl.semaphore_wait(barrier, len(others) + len(slots))

    copies = []
    for k, other in enumerate(others):
        source = part.at[pl.ds(pl.multiple_of(other * chunk, chunk), chunk)]
        copies.append(send(source, arrived.at[k], (send1, recv1), k, {"row": other}))
    mine = pl.ds(pl.multiple_of(me * chunk, chunk), chunk)
    total = part[mine, :]
    for k, copy in enumerate(copies):
        copy.wait_recv()
        total = total + arrived[k]
    gram[mine, :] = total
    spreads = []
    for k, other in enumerate(others):
        spreads.append(send(gram.at[mine], gram.at[mine], (send2, recv2), k, {"row": other}))
    for copy in spreads:
        copy.wait_recv()
    for copy in copies + spreads:
        copy.wait_send()
    own = gram[...]
    solved = iterate(own)
    basis[...] = solved
    if not final:
        return
    squares = jnp.sum(solved * product3(halves(own), halves(solved)), axis=0, keepdims=True)
    squares_ref[...] = squares
    sent, landed, send3, recv3 = refs[5:]
    sent[...] = jnp.broadcast_to(jnp.sum(squares), sent.shape)
    traces = []
    for k, slot in enumerate(slots):
        traces.append(send(sent, landed.at[k], (send3, recv3), k, {"pair": slot}))
    value = sent[...]
    for k, copy in enumerate(traces):
        copy.wait_recv()
        value = value + landed[k]
    total_ref[...] = value
    for copy in traces:
        copy.wait_send()


def solve(part, final):
    n, n_pair = lax.axis_size("row"), lax.axis_size("pair")
    order = part.shape[0]
    dma = pltpu.SemaphoreType.DMA((n - 1,))
    vmem = pl.BlockSpec(memory_space=pltpu.VMEM)
    shapes = [jax.ShapeDtypeStruct(part.shape, jnp.float32)] * 2
    scratch = [pltpu.VMEM((n - 1, order // n, order), jnp.float32), dma, dma, dma, dma]
    if final:
        shapes += [
            jax.ShapeDtypeStruct((1, order), jnp.float32),
            jax.ShapeDtypeStruct((8, 128), jnp.float32),
        ]
        far = pltpu.SemaphoreType.DMA((n_pair - 1,))
        scratch += [
            pltpu.VMEM((8, 128), jnp.float32),
            pltpu.VMEM((n_pair - 1, 8, 128), jnp.float32),
            far,
            far,
        ]
    return pl.pallas_call(
        functools.partial(solve_kernel, n, n_pair, final),
        out_shape=shapes,
        in_specs=[vmem],
        out_specs=[vmem] * len(shapes),
        scratch_shapes=scratch,
        compiler_params=pltpu.CompilerParams(
            collective_id=int(final), has_side_effects=True, vmem_limit_bytes=16 * 1024 * 1024
        ),
        cost_estimate=pl.CostEstimate(
            flops=35 * 6 * order**3, bytes_accessed=40 * 1024 * 1024, transcendentals=0
        ),
    )(part)


def on_device(weight, move_flags):
    half_width = weight.shape[1] // 2
    row_count = weight.shape[0] * lax.axis_size("row")
    cell_count = row_count * weight.shape[1] * lax.axis_size("pair")
    head_rows = weight.shape[0] * 11 // 32
    pieces = [weight[:head_rows], weight[head_rows:]]
    part = contract(weight, weight)
    for round_index in range(ROUNDS):
        final = round_index + 1 == ROUNDS
        if not final:
            behind = from_behind(pieces[0], "pair", 1)
        gram, basis, *sums = solve(part, final)
        if final:
            break
        basis, behind = lax.optimization_barrier((basis, behind))
        lead, tail = basis[:, :half_width], basis[:, half_width:]
        lead_moves = move_flags[round_index, 0] == 1
        mover = jnp.where(lead_moves, lead, tail)
        stayer = jnp.where(lead_moves, tail, lead)
        mover_behind = from_behind(mover, "pair", 1)
        coming = from_behind(times(pieces[1], mover), "pair", 1)
        stays = [times(piece, stayer) for piece in pieces]
        corner = contract(stays[0], stays[0]) + contract(stays[1], stays[1])
        head = jnp.concatenate([stays[0], times(behind, mover_behind)], axis=1)
        edge = contract(head, head[:, half_width:])
        rest = jnp.concatenate([stays[1], coming], axis=1)
        edge = edge + contract(rest, coming)
        pieces = [head, rest]
        part = jnp.concatenate(
            [jnp.concatenate([corner, edge[:half_width].T], axis=0), edge], axis=1
        )
    squares, squares_total = sums[0][0], sums[1][0, 0]
    divisor = jnp.sqrt(squares_total / cell_count)
    current = jnp.concatenate(pieces, axis=0)
    columns = times(current, basis) / divisor
    norm_ratios = jnp.sqrt(squares / row_count) / divisor
    return (columns, norm_ratios)


def solution(mesh):
    return jax.shard_map(
        on_device,
        mesh=mesh,
        in_specs=(P("row", "pair"), P(None, "pair")),
        out_specs=(P("row", "pair"), P("pair")),
        check_vma=False,
    )
```

```python
import functools

import jax
import jax.numpy as jnp
from jax import lax
from jax.experimental import pallas as pl
from jax.experimental.pallas import tpu as pltpu
from jax.sharding import PartitionSpec as P

SWEEPS = 2
POLAR = 8
ROUNDS = 3

MESH = pl.DeviceIdType.MESH
precise = lax.Precision.HIGH


def from_behind(block, axis, distance):
    devices = range(lax.axis_size(axis))
    route = [((i - distance) % len(devices), i) for i in devices]
    return lax.ppermute(block, axis, route)


def contract(left, right):
    return lax.dot_general(
        left, right, (((0,), (0,)), ((), ())), precision=precise, preferred_element_type=jnp.float32
    )


def times(left, right):
    return jnp.dot(left, right, precision=precise, preferred_element_type=jnp.float32)


def halves(value):
    high = value.astype(jnp.bfloat16)
    low = (value - high.astype(jnp.float32)).astype(jnp.bfloat16)
    return high, low


def product3(left, right):
    return jnp.dot(
        jnp.concatenate([left[0], left[0], left[1]], axis=1),
        jnp.concatenate([right[0], right[1], right[0]], axis=0),
        preferred_element_type=jnp.float32,
    )


def iterate(gram):
    gram_parts = halves(gram)
    product = gram
    for sweep in range(SWEEPS):
        if sweep:
            product = product3(gram_parts, halves(product))
        parts = halves(product)
        normal = product3(parts, parts)
        scaled = product / jnp.sqrt(jnp.sqrt(jnp.sum(normal * normal)))

        def step(_, value):
            own = halves(value)
            inner = product3(own, own)
            return 1.5 * value - 0.5 * product3(own, halves(inner))

        product = lax.fori_loop(0, POLAR, step, scaled, unroll=4)
    return product


def send(source, target, semaphores, index, device):
    copy = pltpu.make_async_remote_copy(
        src_ref=source,
        dst_ref=target,
        send_sem=semaphores[0].at[index],
        recv_sem=semaphores[1].at[index],
        device_id=device,
        device_id_type=MESH,
    )
    copy.start()
    return copy


def solve_kernel(n, n_pair, final, corner, edge, gram, basis, *refs):
    if final:
        squares_ref, total_ref = refs[:2]
        refs = refs[2:]
    packed, arrived, sums, both, send1, recv1, send2, recv2, send3, recv3 = refs[:10]
    block = corner.shape[0]
    upper = block // 2
    me = lax.axis_index("row")
    core, chip, n_chips = lax.rem(me, 2), me // 2, n // 2
    twin = me + 1 - 2 * core
    chips = [lax.rem(chip + k, n_chips) for k in range(1, n_chips)]
    peers = [2 * other + core for other in chips]
    pair = lax.axis_index("pair")
    slots = [lax.rem(pair + k, n_pair) for k in range(1, n_pair)] if final else []

    barrier = pltpu.get_barrier_semaphore()
    for other in [twin] + peers:
        pl.semaphore_signal(barrier, inc=1, device_id={"row": other}, device_id_type=MESH)
    for slot in slots:
        pl.semaphore_signal(barrier, inc=1, device_id={"pair": slot}, device_id_type=MESH)
    packed[0, :block] = corner[...]
    packed[0, block:] = edge[:upper]
    packed[1, :block] = edge[block:]
    packed[1, block:] = edge[upper:block]
    pl.semaphore_wait(barrier, n_chips + len(slots))

    first = send(packed.at[1 - core], arrived, (send1, recv1), 0, {"row": twin})
    first.wait_recv()
    sums[chip] = packed[core] + arrived[...]
    copies = []
    for k, peer in enumerate(peers):
        copies.append(send(sums.at[chip], sums.at[chip], (send2, recv2), k, {"row": peer}))
    for copy in copies:
        copy.wait_recv()
    total = sums[0]
    for k in range(1, n_chips):
        total = total + sums[k]
    both[core] = total
    last = send(both.at[core], both.at[core], (send3, recv3), 0, {"row": twin})
    last.wait_recv()
    for copy in [first, last] + copies:
        copy.wait_send()
    cross = jnp.concatenate([both[0, block:], both[1, block:]], axis=0)
    gram[:block, :block] = both[0, :block]
    gram[block:, block:] = both[1, :block]
    gram[:block, block:] = cross
    gram[block:, :block] = cross.T
    own = gram[...]
    solved = iterate(own)
    basis[...] = solved
    if not final:
        return
    squares = jnp.sum(solved * product3(halves(own), halves(solved)), axis=0, keepdims=True)
    squares_ref[...] = squares
    sent, landed, send4, recv4 = refs[10:]
    sent[...] = jnp.broadcast_to(jnp.sum(squares), sent.shape)
    traces = []
    for k, slot in enumerate(slots):
        traces.append(send(sent, landed.at[k], (send4, recv4), k, {"pair": slot}))
    value = sent[...]
    for k, copy in enumerate(traces):
        copy.wait_recv()
        value = value + landed[k]
    total_ref[...] = value
    for copy in traces:
        copy.wait_send()


def solve(corner, edge, final):
    n, n_pair = lax.axis_size("row"), lax.axis_size("pair")
    order = edge.shape[0]
    one, many = pltpu.SemaphoreType.DMA((1,)), pltpu.SemaphoreType.DMA((n // 2 - 1,))
    share = (order * 3 // 4, order // 2)
    vmem = pl.BlockSpec(memory_space=pltpu.VMEM)
    shapes = [jax.ShapeDtypeStruct((order, order), jnp.float32)] * 2
    scratch = [
        pltpu.VMEM((2, *share), jnp.float32),
        pltpu.VMEM(share, jnp.float32),
        pltpu.VMEM((n // 2, *share), jnp.float32),
        pltpu.VMEM((2, *share), jnp.float32),
        one,
        one,
        many,
        many,
        one,
        one,
    ]
    if final:
        shapes += [
            jax.ShapeDtypeStruct((1, order), jnp.float32),
            jax.ShapeDtypeStruct((8, 128), jnp.float32),
        ]
        far = pltpu.SemaphoreType.DMA((n_pair - 1,))
        scratch += [
            pltpu.VMEM((8, 128), jnp.float32),
            pltpu.VMEM((n_pair - 1, 8, 128), jnp.float32),
            far,
            far,
        ]
    return pl.pallas_call(
        functools.partial(solve_kernel, n, n_pair, final),
        out_shape=shapes,
        in_specs=[vmem, vmem],
        out_specs=[vmem] * len(shapes),
        scratch_shapes=scratch,
        compiler_params=pltpu.CompilerParams(
            collective_id=int(final), has_side_effects=True, vmem_limit_bytes=16 * 1024 * 1024
        ),
        cost_estimate=pl.CostEstimate(
            flops=35 * 6 * order**3, bytes_accessed=40 * 1024 * 1024, transcendentals=0
        ),
    )(corner, edge)


def on_device(weight, move_flags):
    half_width = weight.shape[1] // 2
    row_count = weight.shape[0] * lax.axis_size("row")
    cell_count = row_count * weight.shape[1] * lax.axis_size("pair")
    head_rows = weight.shape[0] * 10 // 32
    pieces = [weight[:head_rows], weight[head_rows:]]
    part = contract(weight, weight)
    corner, edge = part[:half_width, :half_width], part[:, half_width:]
    for round_index in range(ROUNDS):
        final = round_index + 1 == ROUNDS
        if not final:
            behind = from_behind(pieces[0], "pair", 1)
        gram, basis, *sums = solve(corner, edge, final)
        if final:
            break
        basis, behind = lax.optimization_barrier((basis, behind))
        lead, tail = basis[:, :half_width], basis[:, half_width:]
        lead_moves = move_flags[round_index, 0] == 1
        mover = jnp.where(lead_moves, lead, tail)
        stayer = jnp.where(lead_moves, tail, lead)
        mover_behind = from_behind(mover, "pair", 1)
        coming = from_behind(times(pieces[1], mover), "pair", 1)
        stays = [times(piece, stayer) for piece in pieces]
        corner = contract(stays[0], stays[0]) + contract(stays[1], stays[1])
        head = jnp.concatenate([stays[0], times(behind, mover_behind)], axis=1)
        edge = contract(head, head[:, half_width:])
        rest = jnp.concatenate([stays[1], coming], axis=1)
        edge = edge + contract(rest, coming)
        pieces = [head, rest]
    squares, squares_total = sums[0][0], sums[1][0, 0]
    divisor = jnp.sqrt(squares_total / cell_count)
    current = jnp.concatenate(pieces, axis=0)
    columns = times(current, basis) / divisor
    norm_ratios = jnp.sqrt(squares / row_count) / divisor
    return (columns, norm_ratios)


def solution(mesh):
    return jax.shard_map(
        on_device,
        mesh=mesh,
        in_specs=(P("row", "pair"), P(None, "pair")),
        out_specs=(P("row", "pair"), P("pair")),
        check_vma=False,
    )
```

```python
import functools

import jax
import jax.numpy as jnp
from jax import lax
from jax.experimental import pallas as pl
from jax.experimental.pallas import tpu as pltpu
from jax.sharding import PartitionSpec as P

SWEEPS = 2
POLAR = 8
ROUNDS = 3

MESH = pl.DeviceIdType.MESH
precise = lax.Precision.HIGH


def from_behind(block, axis, distance):
    devices = range(lax.axis_size(axis))
    route = [((i - distance) % len(devices), i) for i in devices]
    return lax.ppermute(block, axis, route)


def contract(left, right):
    return lax.dot_general(
        left, right, (((0,), (0,)), ((), ())), precision=precise, preferred_element_type=jnp.float32
    )


def times(left, right):
    return jnp.dot(left, right, precision=precise, preferred_element_type=jnp.float32)


def halves(value):
    high = value.astype(jnp.bfloat16)
    low = (value - high.astype(jnp.float32)).astype(jnp.bfloat16)
    return high, low


def product3(left, right):
    return jnp.dot(
        jnp.concatenate([left[0], left[0], left[1]], axis=1),
        jnp.concatenate([right[0], right[1], right[0]], axis=0),
        preferred_element_type=jnp.float32,
    )


def iterate(gram):
    gram_parts = halves(gram)
    product = gram
    for sweep in range(SWEEPS):
        if sweep:
            product = product3(gram_parts, halves(product))
        parts = halves(product)
        normal = product3(parts, parts)
        scaled = product / jnp.sqrt(jnp.sqrt(jnp.sum(normal * normal)))

        def step(_, value):
            own = halves(value)
            inner = product3(own, own)
            return 1.5 * value - 0.5 * product3(own, halves(inner))

        product = lax.fori_loop(0, POLAR, step, scaled, unroll=4)
    return product


def send(source, target, semaphores, index, device):
    copy = pltpu.make_async_remote_copy(
        src_ref=source,
        dst_ref=target,
        send_sem=semaphores[0].at[index],
        recv_sem=semaphores[1].at[index],
        device_id=device,
        device_id_type=MESH,
    )
    copy.start()
    return copy


def solve_kernel(n, n_pair, final, counts, corner, edge, gram, basis, *refs):
    if final:
        norms_ref = refs[0]
        refs = refs[1:]
    packed, arrived, sums, both, send1, recv1, send2, recv2, send3, recv3 = refs[:10]
    block = corner.shape[0]
    upper = block // 2
    me = lax.axis_index("row")
    core, chip, n_chips = lax.rem(me, 2), me // 2, n // 2
    twin = me + 1 - 2 * core
    chips = [lax.rem(chip + k, n_chips) for k in range(1, n_chips)]
    peers = [2 * other + core for other in chips]
    pair = lax.axis_index("pair")
    slots = [lax.rem(pair + k, n_pair) for k in range(1, n_pair)] if final else []

    barrier = pltpu.get_barrier_semaphore()
    for other in [twin] + peers:
        pl.semaphore_signal(barrier, inc=1, device_id={"row": other}, device_id_type=MESH)
    for slot in slots:
        pl.semaphore_signal(barrier, inc=1, device_id={"pair": slot}, device_id_type=MESH)
    packed[0, :block] = corner[...]
    packed[0, block:] = edge[:upper]
    packed[1, :block] = edge[block:]
    packed[1, block:] = edge[upper:block]
    pl.semaphore_wait(barrier, n_chips + len(slots))

    first = send(packed.at[1 - core], arrived, (send1, recv1), 0, {"row": twin})
    first.wait_recv()
    sums[chip] = packed[core] + arrived[...]
    copies = []
    for k, peer in enumerate(peers):
        copies.append(send(sums.at[chip], sums.at[chip], (send2, recv2), k, {"row": peer}))
    for copy in copies:
        copy.wait_recv()
    total = sums[0]
    for k in range(1, n_chips):
        total = total + sums[k]
    both[core] = total
    last = send(both.at[core], both.at[core], (send3, recv3), 0, {"row": twin})
    last.wait_recv()
    for copy in [first, last] + copies:
        copy.wait_send()
    cross = jnp.concatenate([both[0, block:], both[1, block:]], axis=0)
    gram[:block, :block] = both[0, :block]
    gram[block:, block:] = both[1, :block]
    gram[:block, block:] = cross
    gram[block:, :block] = cross.T
    own = gram[...]
    solved = iterate(own)
    if not final:
        basis[...] = solved
        return
    squares = jnp.sum(solved * product3(halves(own), halves(solved)), axis=0, keepdims=True)
    sent, landed, send4, recv4 = refs[10:]
    sent[...] = jnp.broadcast_to(jnp.sum(squares), sent.shape)
    traces = []
    for k, slot in enumerate(slots):
        traces.append(send(sent, landed.at[k], (send4, recv4), k, {"pair": slot}))
    value = sent[...]
    for k, copy in enumerate(traces):
        copy.wait_recv()
        value = value + landed[k]
    row_count, cell_count = counts
    divisor = jnp.sqrt(value[:1, :1] / cell_count)
    basis[...] = solved / divisor
    norms_ref[...] = jnp.sqrt(squares / row_count) / divisor
    for copy in traces:
        copy.wait_send()


def solve(corner, edge, final, counts):
    n, n_pair = lax.axis_size("row"), lax.axis_size("pair")
    order = edge.shape[0]
    one, many = pltpu.SemaphoreType.DMA((1,)), pltpu.SemaphoreType.DMA((n // 2 - 1,))
    share = (order * 3 // 4, order // 2)
    vmem = pl.BlockSpec(memory_space=pltpu.VMEM)
    shapes = [jax.ShapeDtypeStruct((order, order), jnp.float32)] * 2
    scratch = [
        pltpu.VMEM((2, *share), jnp.float32),
        pltpu.VMEM(share, jnp.float32),
        pltpu.VMEM((n // 2, *share), jnp.float32),
        pltpu.VMEM((2, *share), jnp.float32),
        one,
        one,
        many,
        many,
        one,
        one,
    ]
    if final:
        shapes += [jax.ShapeDtypeStruct((1, order), jnp.float32)]
        far = pltpu.SemaphoreType.DMA((n_pair - 1,))
        scratch += [
            pltpu.VMEM((8, 128), jnp.float32),
            pltpu.VMEM((n_pair - 1, 8, 128), jnp.float32),
            far,
            far,
        ]
    return pl.pallas_call(
        functools.partial(solve_kernel, n, n_pair, final, counts),
        out_shape=shapes,
        in_specs=[vmem, vmem],
        out_specs=[vmem] * len(shapes),
        scratch_shapes=scratch,
        compiler_params=pltpu.CompilerParams(
            collective_id=int(final), has_side_effects=True, vmem_limit_bytes=16 * 1024 * 1024
        ),
        cost_estimate=pl.CostEstimate(
            flops=35 * 6 * order**3, bytes_accessed=40 * 1024 * 1024, transcendentals=0
        ),
    )(corner, edge)


def on_device(weight, move_flags):
    half_width = weight.shape[1] // 2
    row_count = weight.shape[0] * lax.axis_size("row")
    counts = (row_count, row_count * weight.shape[1] * lax.axis_size("pair"))
    head_rows = weight.shape[0] * 11 // 32
    pieces = [weight[:head_rows], weight[head_rows:]]
    part = contract(weight, weight)
    corner, edge = part[:half_width, :half_width], part[:, half_width:]
    for round_index in range(ROUNDS):
        final = round_index + 1 == ROUNDS
        if not final:
            behind = from_behind(pieces[0], "pair", 1)
        gram, basis, *sums = solve(corner, edge, final, counts)
        if final:
            break
        lead, tail = basis[:, :half_width], basis[:, half_width:]
        lead_moves = move_flags[round_index, 0] == 1
        mover = jnp.where(lead_moves, lead, tail)
        stayer = jnp.where(lead_moves, tail, lead)
        mover_behind = from_behind(mover, "pair", 1)
        moving, behind = lax.optimization_barrier((times(pieces[1], mover), behind))
        coming = from_behind(moving, "pair", 1)
        stays = [times(piece, stayer) for piece in pieces]
        corner = contract(stays[0], stays[0]) + contract(stays[1], stays[1])
        head = jnp.concatenate([stays[0], times(behind, mover_behind)], axis=1)
        edge = contract(head, head[:, half_width:])
        rest = jnp.concatenate([stays[1], coming], axis=1)
        edge = edge + contract(rest, coming)
        pieces = [head, rest]
    columns = times(jnp.concatenate(pieces, axis=0), basis)
    norm_ratios = sums[0][0]
    return (columns, norm_ratios)


def solution(mesh):
    return jax.shard_map(
        on_device,
        mesh=mesh,
        in_specs=(P("row", "pair"), P(None, "pair")),
        out_specs=(P("row", "pair"), P("pair")),
        check_vma=False,
    )
```

```python
import functools

import jax
import jax.numpy as jnp
from jax import lax
from jax.experimental import pallas as pl
from jax.experimental.pallas import tpu as pltpu
from jax.sharding import PartitionSpec as P

SWEEPS = 2
POLAR = 8
ROUNDS = 3

MESH = pl.DeviceIdType.MESH
precise = lax.Precision.HIGH


def from_behind(block, axis, distance):
    devices = range(lax.axis_size(axis))
    route = [((i - distance) % len(devices), i) for i in devices]
    return lax.ppermute(block, axis, route)


def contract(left, right):
    return lax.dot_general(
        left, right, (((0,), (0,)), ((), ())), precision=precise, preferred_element_type=jnp.float32
    )


def times(left, right):
    return jnp.dot(left, right, precision=precise, preferred_element_type=jnp.float32)


def halves(value):
    high = value.astype(jnp.bfloat16)
    low = (value - high.astype(jnp.float32)).astype(jnp.bfloat16)
    return high, low


def product3(left, right):
    return jnp.dot(
        jnp.concatenate([left[0], left[0], left[1]], axis=1),
        jnp.concatenate([right[0], right[1], right[0]], axis=0),
        preferred_element_type=jnp.float32,
    )


def iterate(gram):
    gram_parts = halves(gram)
    product = gram
    for sweep in range(SWEEPS):
        if sweep:
            product = product3(gram_parts, halves(product))
        parts = halves(product)
        normal = product3(parts, parts)
        scaled = product / jnp.sqrt(jnp.sqrt(jnp.sum(normal * normal)))

        def step(_, value):
            own = halves(value)
            inner = product3(own, own)
            return 1.5 * value - 0.5 * product3(own, halves(inner))

        product = lax.fori_loop(0, POLAR, step, scaled, unroll=4)
    return product


def send(source, target, semaphores, index, device):
    copy = pltpu.make_async_remote_copy(
        src_ref=source,
        dst_ref=target,
        send_sem=semaphores[0].at[index],
        recv_sem=semaphores[1].at[index],
        device_id=device,
        device_id_type=MESH,
    )
    copy.start()
    return copy


def solve_kernel(n, n_pair, final, counts, corner, edge, gram, basis, *refs):
    if final:
        norms_ref = refs[0]
        refs = refs[1:]
    packed, arrived, sums, both, send1, recv1, send2, recv2, send3, recv3 = refs[:10]
    block = corner.shape[0]
    upper = block // 2
    me = lax.axis_index("row")
    core, chip, n_chips = lax.rem(me, 2), me // 2, n // 2
    twin = me + 1 - 2 * core
    chips = [lax.rem(chip + k, n_chips) for k in range(1, n_chips)]
    peers = [2 * other + core for other in chips]
    pair = lax.axis_index("pair")
    slots = [lax.rem(pair + k, n_pair) for k in range(1, n_pair)] if final else []

    barrier = pltpu.get_barrier_semaphore()
    for other in [twin] + peers:
        pl.semaphore_signal(barrier, inc=1, device_id={"row": other}, device_id_type=MESH)
    for slot in slots:
        pl.semaphore_signal(barrier, inc=1, device_id={"pair": slot}, device_id_type=MESH)
    packed[0, :block] = corner[...]
    packed[0, block:] = edge[:upper]
    packed[1, :block] = edge[block:]
    packed[1, block:] = edge[upper:block]
    pl.semaphore_wait(barrier, n_chips + len(slots))

    first = send(packed.at[1 - core], arrived, (send1, recv1), 0, {"row": twin})
    first.wait_recv()
    sums[chip] = packed[core] + arrived[...]
    copies = []
    for k, peer in enumerate(peers):
        copies.append(send(sums.at[chip], sums.at[chip], (send2, recv2), k, {"row": peer}))
    for copy in copies:
        copy.wait_recv()
    total = sums[0]
    for k in range(1, n_chips):
        total = total + sums[k]
    both[core] = total
    last = send(both.at[core], both.at[core], (send3, recv3), 0, {"row": twin})
    last.wait_recv()
    for copy in [first, last] + copies:
        copy.wait_send()
    cross = jnp.concatenate([both[0, block:], both[1, block:]], axis=0)
    gram[:block, :block] = both[0, :block]
    gram[block:, block:] = both[1, :block]
    gram[:block, block:] = cross
    gram[block:, :block] = cross.T
    own = gram[...]
    solved = iterate(own)
    if not final:
        basis[...] = solved
        return
    squares = jnp.sum(solved * product3(halves(own), halves(solved)), axis=0, keepdims=True)
    sent, landed, send4, recv4 = refs[10:]
    sent[...] = jnp.broadcast_to(jnp.sum(squares), sent.shape)
    traces = []
    for k, slot in enumerate(slots):
        traces.append(send(sent, landed.at[k], (send4, recv4), k, {"pair": slot}))
    value = sent[...]
    for k, copy in enumerate(traces):
        copy.wait_recv()
        value = value + landed[k]
    row_count, cell_count = counts
    divisor = jnp.sqrt(value[:1, :1] / cell_count)
    basis[...] = solved / divisor
    norms_ref[...] = jnp.sqrt(squares / row_count) / divisor
    for copy in traces:
        copy.wait_send()


def solve(corner, edge, final, counts):
    n, n_pair = lax.axis_size("row"), lax.axis_size("pair")
    order = edge.shape[0]
    one, many = pltpu.SemaphoreType.DMA((1,)), pltpu.SemaphoreType.DMA((n // 2 - 1,))
    share = (order * 3 // 4, order // 2)
    vmem = pl.BlockSpec(memory_space=pltpu.VMEM)
    shapes = [jax.ShapeDtypeStruct((order, order), jnp.float32)] * 2
    scratch = [
        pltpu.VMEM((2, *share), jnp.float32),
        pltpu.VMEM(share, jnp.float32),
        pltpu.VMEM((n // 2, *share), jnp.float32),
        pltpu.VMEM((2, *share), jnp.float32),
        one,
        one,
        many,
        many,
        one,
        one,
    ]
    if final:
        shapes += [jax.ShapeDtypeStruct((1, order), jnp.float32)]
        far = pltpu.SemaphoreType.DMA((n_pair - 1,))
        scratch += [
            pltpu.VMEM((8, 128), jnp.float32),
            pltpu.VMEM((n_pair - 1, 8, 128), jnp.float32),
            far,
            far,
        ]
    return pl.pallas_call(
        functools.partial(solve_kernel, n, n_pair, final, counts),
        out_shape=shapes,
        in_specs=[vmem, vmem],
        out_specs=[vmem] * len(shapes),
        scratch_shapes=scratch,
        compiler_params=pltpu.CompilerParams(
            collective_id=int(final), has_side_effects=True, vmem_limit_bytes=16 * 1024 * 1024
        ),
        cost_estimate=pl.CostEstimate(
            flops=35 * 6 * order**3, bytes_accessed=40 * 1024 * 1024, transcendentals=0
        ),
    )(corner, edge)


def on_device(weight, move_flags):
    half_width = weight.shape[1] // 2
    row_count = weight.shape[0] * lax.axis_size("row")
    counts = (row_count, row_count * weight.shape[1] * lax.axis_size("pair"))
    head_rows = weight.shape[0] * 11 // 32
    pieces = [weight[:head_rows], weight[head_rows:]]
    first, second = weight[:, :half_width], weight[:, half_width:]
    corner, edge = contract(first, first), contract(weight, second)
    for round_index in range(ROUNDS):
        final = round_index + 1 == ROUNDS
        if not final:
            behind = from_behind(pieces[0], "pair", 1)
        gram, basis, *sums = solve(corner, edge, final, counts)
        if final:
            break
        lead, tail = basis[:, :half_width], basis[:, half_width:]
        lead_moves = move_flags[round_index, 0] == 1
        mover = jnp.where(lead_moves, lead, tail)
        stayer = jnp.where(lead_moves, tail, lead)
        mover_behind = from_behind(mover, "pair", 1)
        moving, behind = lax.optimization_barrier((times(pieces[1], mover), behind))
        coming = from_behind(moving, "pair", 1)
        stays = [times(piece, stayer) for piece in pieces]
        corner = contract(stays[0], stays[0]) + contract(stays[1], stays[1])
        head = jnp.concatenate([stays[0], times(behind, mover_behind)], axis=1)
        edge = contract(head, head[:, half_width:])
        rest = jnp.concatenate([stays[1], coming], axis=1)
        edge = edge + contract(rest, coming)
        pieces = [head, rest]
    columns = times(jnp.concatenate(pieces, axis=0), basis)
    norm_ratios = sums[0][0]
    return (columns, norm_ratios)


def solution(mesh):
    return jax.shard_map(
        on_device,
        mesh=mesh,
        in_specs=(P("row", "pair"), P(None, "pair")),
        out_specs=(P("row", "pair"), P("pair")),
        check_vma=False,
    )
```

```python
import functools

import jax
import jax.numpy as jnp
from jax import lax
from jax.experimental import pallas as pl
from jax.experimental.pallas import tpu as pltpu
from jax.sharding import PartitionSpec as P

SWEEPS = 2
POLAR = 8
ROUNDS = 3

MESH = pl.DeviceIdType.MESH
precise = lax.Precision.HIGH


def from_behind(block, axis, distance):
    devices = range(lax.axis_size(axis))
    route = [((i - distance) % len(devices), i) for i in devices]
    return lax.ppermute(block, axis, route)


def contract(left, right):
    return lax.dot_general(
        left, right, (((0,), (0,)), ((), ())), precision=precise, preferred_element_type=jnp.float32
    )


def times(left, right):
    return jnp.dot(left, right, precision=precise, preferred_element_type=jnp.float32)


def halves(value):
    high = value.astype(jnp.bfloat16)
    low = (value - high.astype(jnp.float32)).astype(jnp.bfloat16)
    return high, low


def product3(left, right):
    return jnp.dot(
        jnp.concatenate([left[0], left[0], left[1]], axis=1),
        jnp.concatenate([right[0], right[1], right[0]], axis=0),
        preferred_element_type=jnp.float32,
    )


def iterate(gram):
    gram_parts = halves(gram)
    product = gram
    for sweep in range(SWEEPS):
        if sweep:
            product = product3(gram_parts, halves(product))
        parts = halves(product)
        normal = product3(parts, parts)
        scaled = product / jnp.sqrt(jnp.sqrt(jnp.sum(normal * normal)))

        def step(_, value):
            own = halves(value)
            inner = product3(own, own)
            return 1.5 * value - 0.5 * product3(own, halves(inner))

        product = lax.fori_loop(0, POLAR, step, scaled, unroll=4)
    return product


def send(source, target, semaphores, index, device):
    copy = pltpu.make_async_remote_copy(
        src_ref=source,
        dst_ref=target,
        send_sem=semaphores[0].at[index],
        recv_sem=semaphores[1].at[index],
        device_id=device,
        device_id_type=MESH,
    )
    copy.start()
    return copy


def solve_kernel(n, n_pair, final, counts, corner, edge, gram, basis, *refs):
    if final:
        norms_ref = refs[0]
        refs = refs[1:]
    packed, arrived, sums, both, send1, recv1, send2, recv2, send3, recv3 = refs[:10]
    block = corner.shape[0]
    upper = block // 2
    me = lax.axis_index("row")
    core, chip, n_chips = lax.rem(me, 2), me // 2, n // 2
    twin = me + 1 - 2 * core
    chips = [lax.rem(chip + k, n_chips) for k in range(1, n_chips)]
    peers = [2 * other + core for other in chips]
    pair = lax.axis_index("pair")
    slots = [lax.rem(pair + k, n_pair) for k in range(1, n_pair)] if final else []

    barrier = pltpu.get_barrier_semaphore()
    for other in [twin] + peers:
        pl.semaphore_signal(barrier, inc=1, device_id={"row": other}, device_id_type=MESH)
    for slot in slots:
        pl.semaphore_signal(barrier, inc=1, device_id={"pair": slot}, device_id_type=MESH)
    packed[0, :block] = corner[...]
    packed[0, block:] = edge[:upper]
    packed[1, :block] = edge[block:]
    packed[1, block:] = edge[upper:block]
    pl.semaphore_wait(barrier, n_chips + len(slots))

    first = send(packed.at[1 - core], arrived, (send1, recv1), 0, {"row": twin})
    first.wait_recv()
    sums[chip] = packed[core] + arrived[...]
    copies = []
    for k, peer in enumerate(peers):
        copies.append(send(sums.at[chip], sums.at[chip], (send2, recv2), k, {"row": peer}))
    for copy in copies:
        copy.wait_recv()
    total = sums[0]
    for k in range(1, n_chips):
        total = total + sums[k]
    both[core] = total
    last = send(both.at[core], both.at[core], (send3, recv3), 0, {"row": twin})
    last.wait_recv()
    for copy in [first, last] + copies:
        copy.wait_send()
    cross = jnp.concatenate([both[0, block:], both[1, block:]], axis=0)
    gram[:block, :block] = both[0, :block]
    gram[block:, block:] = both[1, :block]
    gram[:block, block:] = cross
    gram[block:, :block] = cross.T
    own = gram[...]
    solved = iterate(own)
    if not final:
        basis[...] = solved
        return
    squares = jnp.sum(solved * product3(halves(own), halves(solved)), axis=0, keepdims=True)
    sent, landed, send4, recv4 = refs[10:]
    sent[...] = jnp.broadcast_to(jnp.sum(squares), sent.shape)
    traces = []
    for k, slot in enumerate(slots):
        traces.append(send(sent, landed.at[k], (send4, recv4), k, {"pair": slot}))
    value = sent[...]
    for k, copy in enumerate(traces):
        copy.wait_recv()
        value = value + landed[k]
    row_count, cell_count = counts
    divisor = jnp.sqrt(value[:1, :1] / cell_count)
    basis[...] = solved / divisor
    norms_ref[...] = jnp.sqrt(squares / row_count) / divisor
    for copy in traces:
        copy.wait_send()


def solve(corner, edge, final, counts):
    n, n_pair = lax.axis_size("row"), lax.axis_size("pair")
    order = edge.shape[0]
    one, many = pltpu.SemaphoreType.DMA((1,)), pltpu.SemaphoreType.DMA((n // 2 - 1,))
    share = (order * 3 // 4, order // 2)
    vmem = pl.BlockSpec(memory_space=pltpu.VMEM)
    shapes = [jax.ShapeDtypeStruct((order, order), jnp.float32)] * 2
    scratch = [
        pltpu.VMEM((2, *share), jnp.float32),
        pltpu.VMEM(share, jnp.float32),
        pltpu.VMEM((n // 2, *share), jnp.float32),
        pltpu.VMEM((2, *share), jnp.float32),
        one,
        one,
        many,
        many,
        one,
        one,
    ]
    if final:
        shapes += [jax.ShapeDtypeStruct((1, order), jnp.float32)]
        far = pltpu.SemaphoreType.DMA((n_pair - 1,))
        scratch += [
            pltpu.VMEM((8, 128), jnp.float32),
            pltpu.VMEM((n_pair - 1, 8, 128), jnp.float32),
            far,
            far,
        ]
    return pl.pallas_call(
        functools.partial(solve_kernel, n, n_pair, final, counts),
        out_shape=shapes,
        in_specs=[vmem, vmem],
        out_specs=[vmem] * len(shapes),
        scratch_shapes=scratch,
        compiler_params=pltpu.CompilerParams(
            collective_id=int(final), has_side_effects=True, vmem_limit_bytes=16 * 1024 * 1024
        ),
        cost_estimate=pl.CostEstimate(
            flops=35 * 6 * order**3, bytes_accessed=40 * 1024 * 1024, transcendentals=0
        ),
    )(corner, edge)


def on_device(weight, move_flags):
    half_width = weight.shape[1] // 2
    row_count = weight.shape[0] * lax.axis_size("row")
    counts = (row_count, row_count * weight.shape[1] * lax.axis_size("pair"))
    head_rows = weight.shape[0] * 11 // 32
    pieces = [weight[:head_rows], weight[head_rows:]]
    part = contract(weight, weight)
    corner, edge = part[:half_width, :half_width], part[:, half_width:]
    for round_index in range(ROUNDS):
        final = round_index + 1 == ROUNDS
        if not final:
            behind = from_behind(pieces[0], "pair", 1)
        gram, basis, *sums = solve(corner, edge, final, counts)
        if final:
            break
        lead, tail = basis[:, :half_width], basis[:, half_width:]
        lead_moves = move_flags[round_index, 0] == 1
        mover = jnp.where(lead_moves, lead, tail)
        stayer = jnp.where(lead_moves, tail, lead)
        mover_behind = from_behind(mover, "pair", 1)
        moving, behind, stayer = lax.optimization_barrier(
            (times(pieces[1], mover), behind, stayer)
        )
        coming = from_behind(moving, "pair", 1)
        stays = [times(piece, stayer) for piece in pieces]
        corner = contract(stays[0], stays[0]) + contract(stays[1], stays[1])
        head = jnp.concatenate([stays[0], times(behind, mover_behind)], axis=1)
        edge = contract(head, head[:, half_width:])
        rest = jnp.concatenate([stays[1], coming], axis=1)
        edge = edge + contract(rest, coming)
        pieces = [head, rest]
    columns = times(jnp.concatenate(pieces, axis=0), basis)
    norm_ratios = sums[0][0]
    return (columns, norm_ratios)


def solution(mesh):
    return jax.shard_map(
        on_device,
        mesh=mesh,
        in_specs=(P("row", "pair"), P(None, "pair")),
        out_specs=(P("row", "pair"), P("pair")),
        check_vma=False,
    )
```
